512 devices in a mesh: inner: 16 (over z_hi, x, core), outer: 32 (over z_lo, y).
Axes of the slice: x: 4, y: 4, z: 16 (z_hi: 2, z_lo: 8; z = z_hi * 8 + z_lo), core: 2. Of those that a mesh axis runs over, the one named last changes fastest.
Arguments:
- centres: float32 [3, 262144], P(None, ('outer', 'inner')), may hold values from -1 to 1
- leaf_order: int32 [512, 512], P(('outer', 'inner')), may hold values from 0 to 511, each once within a row
- nugget: float32 [262144], P(('outer', 'inner')), may hold values from 0.5 to 2
- left_fine: bfloat16 [4, 64, 262144], P(None, None, ('outer', 'inner')), may hold values from -0.75 to 0.75
- right_fine: bfloat16 [4, 64, 262144], P(None, None, ('outer', 'inner')), may hold values from -0.133466405 to 0.133466405
- left_coarse: bfloat16 [5, 64, 262144], P(None, None, ('outer', 'inner')), may hold values from -0.75 to 0.75
- right_coarse: bfloat16 [5, 64, 262144], P(None, None, ('outer', 'inner')), may hold values from -0.033366601 to 0.033366601
- right_sides: float32 [48, 262144], P(None, ('outer', 'inner')), may hold values from -320 to 320
Outputs:
- next_basis: float32 [48, 262144], P(None, ('outer', 'inner'))
- hessenberg: float32 [48, 5, 4], replicated
The draws below stay inside these ranges and needn't reach their ends.
Inputs may be any that keep to these rules, and one draw needn't show every extreme that they name: `leaf_order`: each row is an order of 0 to 511, each number once.
All inputs are finite; a program needn't handle non-finite values.
Results may differ from the reference program's by a relative error of at most 0.0037.
Values sent between devices are 32-bit elements; how exact they have to be, the bound alone decides.
A program may use at most 64 MiB of HBM per device.

```python
import math
import jax
import jax.numpy as jnp
from jax import lax

ROWS = 512
RANK = 64
NRHS = 48
STEPS = 4
LEV_IN = 4
LEV_OUT = 5
BLOCKS = 512
ORDER = 262144
N_INNER = 16
N_OUTER = 32


def level_scaled(values, first):
    level_ids = first + jnp.arange(values.shape[0]).astype(jnp.float32)
    factor = 1.0 / jnp.sqrt(ROWS * jnp.exp2(level_ids))
    return (values * factor[:, None, None]).astype(jnp.bfloat16)


def rising_factor(log_rise):
    blocks = ORDER // ROWS
    inner_count = 2 ** LEV_IN
    block_ids = jnp.arange(ORDER, dtype=jnp.int32) // ROWS
    outer_ids = block_ids // inner_count
    inner_ids = block_ids % inner_count
    position = (inner_ids * (blocks // inner_count) + outer_ids).astype(jnp.float32) / float(blocks - 1)
    return jnp.exp(position * log_rise)


def draw_right_fine(key, part):
    key = jax.random.fold_in(key, 5)
    shape = (LEV_IN, RANK, ORDER)
    values = jax.random.truncated_normal(key, -3.0, 3.0, shape, jnp.float32)
    return level_scaled(values, 0.0)


def draw_right_coarse(key, part):
    key = jax.random.fold_in(key, 9)
    shape = (LEV_OUT, RANK, ORDER)
    values = jax.random.truncated_normal(key, -3.0, 3.0, shape, jnp.float32)
    return level_scaled(values, float(LEV_IN))


def draw_right_sides(key, part):
    key = jax.random.fold_in(key, 13)
    scale_key, value_key = jax.random.split(key)
    shape = (NRHS, ORDER)
    scales = jnp.exp(jax.random.uniform(scale_key, shape, jnp.float32, 0.0, 2.302585))
    values = jax.random.truncated_normal(value_key, -4.0, 4.0, shape, jnp.float32) * scales * rising_factor(1.791759)[None, :]
    return values


def block_scale(stream_key, shape, cuts, least, high):
    level = 1.0
    for dim, blocks in cuts:
        steps = jax.random.uniform(jax.random.fold_in(jax.random.fold_in(stream_key, 6), dim), (blocks,), jnp.float32, least / len(cuts), high / len(cuts))
        level = level * jnp.repeat(jnp.exp(steps), shape[dim] // blocks).reshape((-1,) + (1,) * (len(shape) - 1 - dim))
    return level


def gaussian(own_key, extent, scale, bound, cuts=(), held_as=jnp.bfloat16):
    loudness = block_scale(own_key, extent, cuts, -0.22, 0.18) if cuts else 1.0
    entries = jax.random.normal(own_key, extent, jnp.float32) * scale * loudness
    return jnp.minimum(jnp.maximum(entries, -bound), bound).astype(held_as)


def setup_inputs(seed: int = 0) -> dict:
    key_list = jax.random.split(jax.random.key(seed), 9)
    return {
        "centres": jnp.clip(jax.random.uniform(key_list[0], (3, ORDER), jnp.float32, -1.0, 1.0) * block_scale(key_list[0], (3, ORDER), ((1, 512),), -0.4, 0.0), -1.0, 1.0),
        "leaf_order": jax.vmap(lambda own: jax.random.permutation(own, ROWS))(jax.random.split(key_list[1], BLOCKS)).reshape((BLOCKS, ROWS)).astype(jnp.int32),
        "nugget": jnp.clip(jnp.exp(math.log(2.0) - 1.3862944 * jax.random.uniform(key_list[2], (ORDER,), jnp.float32) ** block_scale(key_list[2], (ORDER,), ((0, 512),), -0.2, 0.2)), 0.5, 2.0),
        "left_fine": gaussian(key_list[3], (LEV_IN, RANK, ORDER), RANK ** -0.5, 0.75, ((2, 512),)),
        "right_fine": draw_right_fine(jax.random.fold_in(key_list[8], 71), 0),
        "left_coarse": gaussian(key_list[5], (LEV_OUT, RANK, ORDER), RANK ** -0.5, 0.75, ((2, 512),)),
        "right_coarse": draw_right_coarse(jax.random.fold_in(key_list[8], 71), 0),
        "right_sides": draw_right_sides(jax.random.fold_in(key_list[8], 71), 0),
    }


SHAPE_SQUARED = 0.0625
EPSILON = 1e-06

def kernel_block(points):
    distance = jnp.zeros((points.shape[1], points.shape[1]), jnp.float32)
    for coord in range(3):
        offset = points[coord][:, None] - points[coord][None, :]
        distance = distance + offset * offset
    return (jnp.sqrt(distance + SHAPE_SQUARED) / jnp.sqrt(jnp.float32(ROWS))).astype(jnp.bfloat16)

def dense_one(pair):
    block_points, block_vector = pair
    return jnp.dot(block_vector, kernel_block(block_points), preferred_element_type=jnp.float32)

def reference(centres, leaf_order, nugget, left_fine, right_fine, left_coarse, right_coarse, right_sides):
    blocks = N_INNER * N_OUTER
    order = blocks * ROWS
    levels = LEV_IN + LEV_OUT
    points = jnp.take_along_axis(centres.reshape(3, blocks, ROWS), leaf_order[None].astype(jnp.int32), axis=2)
    points = jnp.transpose(points, (1, 0, 2))
    left_all = jnp.concatenate([left_fine, left_coarse], 0).reshape(levels, RANK, blocks, ROWS)
    right_all = jnp.concatenate([right_fine, right_coarse], 0).reshape(levels, RANK, blocks, ROWS)
    nugget_blocks = nugget.reshape(blocks, ROWS)

    def apply(vector):
        rounded = vector.astype(jnp.bfloat16).reshape(NRHS, blocks, ROWS)
        result = nugget_blocks[None] * vector.reshape(NRHS, blocks, ROWS)
        dense = lax.map(dense_one, (points, jnp.transpose(rounded, (1, 0, 2))))
        result = result + jnp.transpose(dense, (1, 0, 2))
        for level in range(levels):
            terms = jnp.einsum('kbr,nbr->bkn', right_all[level].astype(jnp.float32), rounded.astype(jnp.float32), precision=lax.Precision.HIGHEST)
            width = 2 ** level
            cluster = terms.reshape(blocks // width, width, RANK, NRHS).sum(1)
            sibling = cluster.reshape(blocks // (2 * width), 2, RANK, NRHS)[:, ::-1].reshape(blocks // width, RANK, NRHS)
            sibling = jnp.repeat(sibling, width, axis=0)
            result = result + jnp.einsum('bkn,kbr->nbr', sibling, left_all[level].astype(jnp.float32), precision=lax.Precision.HIGHEST)
        return result.reshape(NRHS, order)
    total = jnp.float32(order)
    start = lax.optimization_barrier(jnp.sum(right_sides * right_sides, axis=1)) / total
    basis = [right_sides / jnp.sqrt(start + EPSILON)[:, None]]
    columns = []
    for step_index in range(STEPS):
        image = apply(basis[-1])
        coeffs = jnp.stack([lax.optimization_barrier(jnp.sum(earlier * image, axis=1)) for earlier in basis]) / total
        for position, earlier in enumerate(basis):
            image = image - coeffs[position][:, None] * earlier
        norm_value = jnp.sqrt(lax.optimization_barrier(jnp.sum(image * image, axis=1)) / total + EPSILON)
        column = jnp.concatenate([coeffs, norm_value[None], jnp.zeros((STEPS - 1 - step_index, NRHS), jnp.float32)], 0)
        columns.append(column)
        basis.append(image / norm_value[:, None])
    hessenberg = jnp.transpose(jnp.stack(columns, 0), (2, 1, 0))
    return (basis[-1], hessenberg)
```

```python
import functools

import jax
import jax.numpy as jnp
from jax import lax
from jax.experimental import pallas as pl
from jax.experimental.pallas import tpu as pltpu
from jax.sharding import PartitionSpec as P

ROWS = 512
RANK = 64
NRHS = 48
STEPS = 4
SLICES = 32
DEPTH = 16
TOTAL = 262144.0
SHAPE_SQUARED = 0.0625
EPSILON = 1e-06
MESH = pl.DeviceIdType.MESH
F32 = jnp.float32
BF16 = jnp.bfloat16


def split(value):
    high = value.astype(BF16)
    low = (value - high.astype(F32)).astype(BF16)
    return jnp.concatenate([high, low], 0)


def joined(value):
    return value[:NRHS] + value[NRHS:]


def dot(left, right):
    return jnp.dot(left, right, preferred_element_type=F32)


def dot_t(left, right):
    return lax.dot_general(left, right, (((1,), (1,)), ((), ())), preferred_element_type=F32)


def total_of(value):
    return jnp.sum(value, axis=1, keepdims=True)


def tree(values):
    values = list(values)
    while len(values) > 1:
        values = [values[i] + values[i + 1] for i in range(0, len(values), 2)]
    return values[0]


def body(
    centres, leaf_order, nugget, left_fine, right_fine, left_coarse, right_coarse, right_sides,
    out, hess,
    c8, order_right, order_left, kernel, tx0, rx0, tx1, rx1, tx2, rx2, txp, rxp, tx3, rx3,
    tx4, rx4, tx5, rx5, send, recv,
):
    inner, outer = lax.axis_index("inner"), lax.axis_index("outer")
    plane = (outer % 4) * 8 + inner % 8

    def plane_peer(d):
        return {"inner": inner ^ (d & 7), "outer": outer ^ (d >> 3)}

    def depth_peer(z):
        return {"inner": inner ^ ((z & 1) << 3), "outer": outer ^ ((z >> 1) << 2)}

    def copy(src, dst, sems, peer):
        return pltpu.make_async_remote_copy(
            src_ref=src, dst_ref=dst, send_sem=send.at[sems], recv_sem=recv.at[sems],
            device_id=peer, device_id_type=MESH,
        )

    barrier = pltpu.get_barrier_semaphore()

    @pl.loop(1, SLICES)
    def _(d):
        pl.semaphore_signal(barrier, inc=1, device_id=plane_peer(d), device_id_type=MESH)

    @pl.loop(1, DEPTH)
    def _(z):
        pl.semaphore_signal(barrier, inc=1, device_id=depth_peer(z), device_id_type=MESH)

    row = lax.broadcasted_iota(jnp.int32, (512, 512), 0)
    col = lax.broadcasted_iota(jnp.int32, (512, 512), 1)
    wanted = (row & 7) * RANK + ((row & 255) >> 3) * 2 + (row >> 8)
    order = jnp.where(wanted == col, 1.0, 0.0).astype(BF16)

    def levels_above(fine, coarse):
        return jnp.concatenate(
            [fine[1:].reshape(3 * RANK, ROWS), coarse[...].reshape(5 * RANK, ROWS)], 0
        )

    order_right[...] = dot(order, levels_above(right_fine, right_coarse)).astype(BF16)

    lane = lax.broadcasted_iota(jnp.int32, (32, 256), 1)
    spare_dot, spare_odd = (lane >> 4) & 7, ((lane >> 3) & 1) == 1
    tile_row = lax.broadcasted_iota(jnp.int32, (8, 128), 0)
    tile_spare = lax.broadcasted_iota(jnp.int32, (8, 128), 1) >= 96

    def start_round(r, vector, dots):
        parts = split(vector)
        terms = joined(dot_t(parts, order_right[...]))
        spare = jnp.zeros((32, 256), F32)
        for i, value in enumerate(dots):
            spare = jnp.where(
                spare_dot == i, jnp.where(spare_odd, value[16:48], value[0:32]), spare
            )
        tiles = jnp.concatenate([terms[:, :256], terms[:, 256:], spare], 0).T
        tx1[r] = tiles.reshape(SLICES, 8, 128)
        if r == 0:
            pl.semaphore_wait(barrier, SLICES + DEPTH - 2)

        @pl.loop(1, SLICES)
        def _(d):
            copy(tx1.at[r, plane ^ d], rx1.at[r, d], (r, 1), plane_peer(d)).start()

        tx0[r] = joined(dot_t(parts, right_fine[0]))
        copy(tx0.at[r], rx0.at[r], (r, 0), plane_peer(1)).start()
        return parts

    def sums_round(r):
        copy(tx1.at[r, pl.ds(1, 31)], rx1.at[r, pl.ds(1, 31)], (r, 1), plane_peer(1)).wait_recv()
        own = tx1[r, plane]
        chip = [own + rx1[r, 1]] + [rx1[r, 2 * e] + rx1[r, 2 * e + 1] for e in range(1, 16)]
        pair = [chip[2 * h] + chip[2 * h + 1] for h in range(8)]
        line = [pair[2 * y] + pair[2 * y + 1] for y in range(4)]
        half = [line[0] + line[1], line[2] + line[3]]
        whole = half[0] + half[1]
        for z in range(3):
            tx2[r, z] = whole[5 + z : 6 + z]
        for m in range(2):
            txp[r, m] = jnp.where(
                tile_row < 5, line[2 * m], pltpu.roll(line[2 * m + 1], 3, axis=0)
            )
        copy(txp.at[r], rxp.at[r], (r, 3), depth_peer(1)).start()

        @pl.loop(2, DEPTH)
        def _(z):
            which = jnp.where(z < 4, 0, jnp.where(z < 8, 1, 2))
            copy(tx2.at[r, which], rx2.at[r, z], (r, 2), depth_peer(z)).start()

        copy(txp.at[r], rxp.at[r], (r, 3), depth_peer(1)).wait_recv()
        rows = rx2.at[r, pl.ds(2, 14)]
        copy(rows, rows, (r, 2), depth_peer(1)).wait_recv()
        far = []
        for m in range(2):
            both = rxp[r, m]
            far += [both, pltpu.roll(both, 5, axis=0)]
        far_half = [far[0] + far[1], far[2] + far[3]]
        six = tree([rx2[r, z] for z in range(2, 4)])
        seven = tree([rx2[r, z] for z in range(4, 8)])
        eight = tree([rx2[r, z] for z in range(8, 16)])
        products = whole[2:3] + (far_half[0] + far_half[1])[2:3]
        products = products + six + seven + eight
        high = jnp.where(tile_row == 5, six, jnp.where(tile_row == 6, seven, eight))
        for y in range(4):
            base = jnp.where(tile_row == 4, half[1 - y // 2] + far_half[1 - y // 2], high)
            base = jnp.where(tile_row == 3, line[y ^ 1] + far[y ^ 1], base)
            base = jnp.where(tile_row == 2, far[y], base)
            for x in range(4):
                e = 4 * y + x
                tile = jnp.where(tile_row == 1, pair[(e // 2) ^ 1], base)
                tile = jnp.where(tile_row == 0, chip[e ^ 1], tile)
                tile = jnp.where(tile_spare, products, tile)
                tx3[r, e] = tile
                if e == 0:
                    rx3[r, plane] = tile

        @pl.loop(1, SLICES)
        def _(d):
            copy(tx3.at[r, d >> 1], rx3.at[r, plane], (r, 4), plane_peer(d)).start()

    def local_part(r, vector, parts):
        part = nugget[...] * vector + joined(dot(parts, kernel[...]))
        copy(tx0.at[r], rx0.at[r], (r, 0), plane_peer(1)).wait_recv()
        return part + joined(dot(split(rx0[r]), left_fine[0]))

    def end_round(r, count):
        slots = rx3.at[r, pl.ds(0, 31)]
        copy(slots, slots, (r, 4), plane_peer(1)).wait_recv()
        turned = rx3[r].reshape(256, 128).T
        sibling = jnp.concatenate([turned[:48], turned[48:96]], 1)
        far = joined(dot(split(sibling), order_left[...]))
        spare = turned[96:]
        return far, [
            jnp.concatenate(
                [spare[:, 16 * i : 16 * i + 1], spare[16:, 16 * i + 8 : 16 * i + 9]], 0
            ) * (1.0 / TOTAL)
            for i in range(count)
        ]

    first = right_sides[...]
    parts = start_round(0, first, [total_of(first * first)])

    order_left[...] = dot(order, levels_above(left_fine, left_coarse)).astype(BF16)
    c8[...] = jnp.zeros_like(c8)
    c8[0:3] = centres[...]
    coords = c8[...]
    c_high = coords.astype(BF16).astype(F32)
    c_mid = (coords - c_high).astype(BF16).astype(F32)
    c_low = coords - c_high - c_mid
    chosen = jnp.where(row == leaf_order[...], 1.0, 0.0).astype(BF16)
    split_coords = jnp.concatenate([c_high, c_mid, c_low, jnp.zeros_like(coords)], 0)
    picked = dot(split_coords.astype(BF16), chosen)
    points = (picked[0:8] + picked[8:16]) + picked[16:24]
    points_t = jnp.concatenate([points, jnp.zeros((120, ROWS), F32)], 0).T
    block = 64
    for start in range(0, ROWS, block):
        distance = jnp.full((block, ROWS), SHAPE_SQUARED, F32)
        for coord in range(3):
            between = points_t[start : start + block, coord : coord + 1] - points[coord : coord + 1]
            distance = distance + between * between
        kernel[start : start + block] = (jnp.sqrt(distance) * (1.0 / ROWS**0.5)).astype(BF16)

    near = local_part(0, first, parts)
    sums_round(0)
    far, (square,) = end_round(0, 1)
    norm = jnp.sqrt(square + EPSILON)
    basis = [first / norm]
    images = [(near + far) / norm]
    gram = [[square / (square + EPSILON)]]
    lanes = lax.broadcasted_iota(jnp.int32, (NRHS, 128), 1)
    table = jnp.zeros((NRHS, 128), F32)

    def orthogonalize(step, dots):
        coeffs, square = dots[:-1], dots[-1]
        count = len(coeffs)
        spread = [sum(gram[i][k] * coeffs[k] for k in range(count)) for i in range(count)]
        for i in range(count):
            square = square - coeffs[i] * (2.0 * coeffs[i] - spread[i])
        square = jnp.maximum(square, 0.0)
        norm = jnp.sqrt(square + EPSILON)
        column = [(coeffs[i] - spread[i]) / norm for i in range(count)]
        for i in range(count):
            gram[i].append(column[i])
        gram.append(column + [square / (square + EPSILON)])
        return coeffs, norm

    def combine(value, coeffs, earlier, norm):
        for coeff, other in zip(coeffs, earlier):
            value = value - coeff * other
        return value / norm

    def record(table, step, coeffs, norm):
        for i, value in enumerate(coeffs + [norm]):
            table = jnp.where(lanes == i * STEPS + step, value, table)
        return table

    for r in range(1, STEPS):
        image = images[-1]
        dots = [total_of(other * image) for other in basis] + [total_of(image * image)]
        parts = start_round(r, image, dots)
        near = local_part(r, image, parts)
        sums_round(r)
        far, dots = end_round(r, len(dots))
        coeffs, norm = orthogonalize(r - 1, dots)
        table = record(table, r - 1, coeffs, norm)
        basis.append(combine(image, coeffs, basis, norm))
        images.append(combine(near + far, coeffs, images, norm))

    image = images[-1]
    dots = [total_of(other * image) for other in basis] + [total_of(image * image)]
    side = jnp.zeros((128, 128), F32)
    lanes_all = lax.broadcasted_iota(jnp.int32, (128, 128), 1)
    zeros = jnp.zeros((32, 1), F32)
    for i in range(3):
        below = dots[2 * i + 1] if i < 2 else jnp.zeros((NRHS, 1), F32)
        side = jnp.where(lanes_all == i, jnp.concatenate([dots[2 * i], below, zeros], 0), side)
    tx4[...] = side.T[:8]

    @pl.loop(1, SLICES)
    def _(d):
        copy(tx4, rx4.at[d], (STEPS, 0), plane_peer(d)).start()

    slots = rx4.at[pl.ds(1, 31)]
    copy(slots, slots, (STEPS, 0), plane_peer(1)).wait_recv()
    tx5[...] = tree([tx4[...]] + [rx4[d] for d in range(1, SLICES)])

    @pl.loop(1, DEPTH)
    def _(z):
        copy(tx5, rx5.at[z], (STEPS, 1), depth_peer(z)).start()

    slots = rx5.at[pl.ds(1, 15)]
    copy(slots, slots, (STEPS, 1), depth_peer(1)).wait_recv()
    summed = tree([tx5[...]] + [rx5[z] for z in range(1, DEPTH)]) * (1.0 / TOTAL)
    side = jnp.concatenate([summed, jnp.zeros((120, 128), F32)], 0).T
    dots = [side[48 * (i % 2) : 48 * (i % 2) + 48, i // 2 : i // 2 + 1] for i in range(5)]
    coeffs, norm = orthogonalize(STEPS - 1, dots)
    hess[...] = record(table, STEPS - 1, coeffs, norm)
    out[...] = combine(image, coeffs, basis, norm)

    for r in range(STEPS):
        copy(tx0.at[r], rx0.at[r], (r, 0), plane_peer(1)).wait_send()
        copy(tx1.at[r, pl.ds(1, 31)], rx1.at[r, pl.ds(1, 31)], (r, 1), plane_peer(1)).wait_send()
        rows = rx2.at[r, pl.ds(2, 14)]
        copy(rows, rows, (r, 2), depth_peer(1)).wait_send()
        copy(txp.at[r], rxp.at[r], (r, 3), depth_peer(1)).wait_send()
        slots = rx3.at[r, pl.ds(0, 31)]
        copy(slots, slots, (r, 4), plane_peer(1)).wait_send()
    slots = rx4.at[pl.ds(1, 31)]
    copy(slots, slots, (STEPS, 0), plane_peer(1)).wait_send()
    slots = rx5.at[pl.ds(1, 15)]
    copy(slots, slots, (STEPS, 1), depth_peer(1)).wait_send()


def on_device(
    centres, leaf_order, nugget, left_fine, right_fine, left_coarse, right_coarse, right_sides
):
    vmem = pl.BlockSpec(memory_space=pltpu.VMEM)
    basis, table = pl.pallas_call(
        body,
        out_shape=(
            jax.ShapeDtypeStruct((NRHS, ROWS), F32),
            jax.ShapeDtypeStruct((NRHS, 128), F32),
        ),
        in_specs=[vmem] * 8,
        out_specs=(vmem, vmem),
        scratch_shapes=[
            pltpu.VMEM((8, ROWS), F32),
            pltpu.VMEM((512, ROWS), BF16),
            pltpu.VMEM((512, ROWS), BF16),
            pltpu.VMEM((ROWS, ROWS), BF16),
            pltpu.VMEM((STEPS, NRHS, RANK), F32),
            pltpu.VMEM((STEPS, NRHS, RANK), F32),
            pltpu.VMEM((STEPS, SLICES, 8, 128), F32),
            pltpu.VMEM((STEPS, SLICES, 8, 128), F32),
            pltpu.VMEM((STEPS, 3, 1, 128), F32),
            pltpu.VMEM((STEPS, DEPTH, 1, 128), F32),
            pltpu.VMEM((STEPS, 2, 8, 128), F32),
            pltpu.VMEM((STEPS, 2, 8, 128), F32),
            pltpu.VMEM((STEPS, 16, 8, 128), F32),
            pltpu.VMEM((STEPS, SLICES, 8, 128), F32),
            pltpu.VMEM((8, 128), F32),
            pltpu.VMEM((SLICES, 8, 128), F32),
            pltpu.VMEM((8, 128), F32),
            pltpu.VMEM((DEPTH, 8, 128), F32),
            pltpu.SemaphoreType.DMA((STEPS + 1, 5)),
            pltpu.SemaphoreType.DMA((STEPS + 1, 5)),
        ],
        compiler_params=pltpu.CompilerParams(
            collective_id=0, has_side_effects=True, vmem_limit_bytes=40 * 1024 * 1024
        ),
    )(
        centres, leaf_order, nugget.reshape(1, ROWS), left_fine, right_fine, left_coarse,
        right_coarse, right_sides,
    )
    hessenberg = table[:, : (STEPS + 1) * STEPS].reshape(NRHS, STEPS + 1, STEPS)
    return (basis, hessenberg)


def solution(mesh):
    return jax.shard_map(
        on_device,
        mesh=mesh,
        in_specs=(
            P(None, ("outer", "inner")),
            P(("outer", "inner"), None),
            P(("outer", "inner")),
            P(None, None, ("outer", "inner")),
            P(None, None, ("outer", "inner")),
            P(None, None, ("outer", "inner")),
            P(None, None, ("outer", "inner")),
            P(None, ("outer", "inner")),
        ),
        out_specs=(P(None, ("outer", "inner")), P()),
        check_vma=False,
    )
```

```python
import functools

import jax
import jax.numpy as jnp
from jax import lax
from jax.experimental import pallas as pl
from jax.experimental.pallas import tpu as pltpu
from jax.sharding import PartitionSpec as P

ROWS = 512
RANK = 64
NRHS = 48
STEPS = 4
SLICES = 32
DEPTH = 16
TOTAL = 262144.0
SHAPE_SQUARED = 0.0625
EPSILON = 1e-06
MESH = pl.DeviceIdType.MESH
F32 = jnp.float32
BF16 = jnp.bfloat16


def split(value):
    high = value.astype(BF16)
    low = (value - high.astype(F32)).astype(BF16)
    return jnp.concatenate([high, low], 0)


def joined(value):
    return value[:NRHS] + value[NRHS:]


def dot(left, right):
    return jnp.dot(left, right, preferred_element_type=F32)


def dot_t(left, right):
    return lax.dot_general(left, right, (((1,), (1,)), ((), ())), preferred_element_type=F32)


def total_of(value):
    return jnp.sum(value, axis=1, keepdims=True)


def tree(values):
    values = list(values)
    while len(values) > 1:
        values = [values[i] + values[i + 1] for i in range(0, len(values), 2)]
    return values[0]


def body(*refs):
    sources, refs = refs[:8], refs[8:]
    out, hess = refs[:2]
    held, refs = refs[2:10], refs[10:]
    centres, leaf_order, nugget, left_fine, right_fine, left_coarse, right_coarse, right_sides = held
    (
        c8, order_right, order_left, kernel, tx0, rx0, tx1, rx1, tx2, rx2, txp, rxp, tx3, rx3,
        tx4, rx4, tx5, rx5, send, recv, fetched,
    ) = refs
    fetches = [
        pltpu.make_async_copy(sources[i], held[i], fetched.at[i]) for i in range(8)
    ]
    for i in (4, 6, 7, 3, 5, 1, 0, 2):
        fetches[i].start()
    inner, outer = lax.axis_index("inner"), lax.axis_index("outer")
    plane = (outer % 4) * 8 + inner % 8

    def plane_peer(d):
        return {"inner": inner ^ (d & 7), "outer": outer ^ (d >> 3)}

    def depth_peer(z):
        return {"inner": inner ^ ((z & 1) << 3), "outer": outer ^ ((z >> 1) << 2)}

    def copy(src, dst, sems, peer):
        return pltpu.make_async_remote_copy(
            src_ref=src, dst_ref=dst, send_sem=send.at[sems], recv_sem=recv.at[sems],
            device_id=peer, device_id_type=MESH,
        )

    barrier = pltpu.get_barrier_semaphore()

    @pl.loop(1, SLICES)
    def _(d):
        pl.semaphore_signal(barrier, inc=1, device_id=plane_peer(d), device_id_type=MESH)

    @pl.loop(1, DEPTH)
    def _(z):
        pl.semaphore_signal(barrier, inc=1, device_id=depth_peer(z), device_id_type=MESH)

    row = lax.broadcasted_iota(jnp.int32, (512, 512), 0)
    col = lax.broadcasted_iota(jnp.int32, (512, 512), 1)
    wanted = (row & 7) * RANK + ((row & 255) >> 3) * 2 + (row >> 8)
    order = jnp.where(wanted == col, 1.0, 0.0).astype(BF16)

    def levels_above(fine, coarse):
        return jnp.concatenate(
            [fine[1:].reshape(3 * RANK, ROWS), coarse[...].reshape(5 * RANK, ROWS)], 0
        )

    fetches[4].wait()
    fetches[6].wait()
    order_right[...] = dot(order, levels_above(right_fine, right_coarse)).T.astype(BF16)

    lane = lax.broadcasted_iota(jnp.int32, (32, 256), 1)
    spare_dot, spare_odd = (lane >> 4) & 7, ((lane >> 3) & 1) == 1
    tile_row = lax.broadcasted_iota(jnp.int32, (8, 128), 0)
    tile_spare = lax.broadcasted_iota(jnp.int32, (8, 128), 1) >= 96

    def start_round(r, vector, dots):
        parts = split(vector)
        terms = joined(dot(parts, order_right[...]))
        spare = jnp.zeros((32, 256), F32)
        for i, value in enumerate(dots):
            spare = jnp.where(
                spare_dot == i, jnp.where(spare_odd, value[16:48], value[0:32]), spare
            )
        tiles = jnp.concatenate([terms[:, :256], terms[:, 256:], spare], 0).T
        tx1[r] = tiles.reshape(SLICES, 8, 128)
        if r == 0:
            prepare()
            pl.semaphore_wait(barrier, SLICES + DEPTH - 2)
        for d in range(SLICES - 1, 0, -1):
            copy(tx1.at[r, plane ^ d], rx1.at[r, d], (r, 1), plane_peer(d)).start()

        tx0[r] = joined(dot_t(parts, right_fine[0]))
        copy(tx0.at[r], rx0.at[r], (r, 0), plane_peer(1)).start()
        return parts

    def sums_round(r):
        copy(tx1.at[r, pl.ds(1, 31)], rx1.at[r, pl.ds(1, 31)], (r, 1), plane_peer(1)).wait_recv()
        own = tx1[r, plane]
        chip = [own + rx1[r, 1]] + [rx1[r, 2 * e] + rx1[r, 2 * e + 1] for e in range(1, 16)]
        pair = [chip[2 * h] + chip[2 * h + 1] for h in range(8)]
        line = [pair[2 * y] + pair[2 * y + 1] for y in range(4)]
        half = [line[0] + line[1], line[2] + line[3]]
        whole = half[0] + half[1]
        for z in range(3):
            tx2[r, z] = whole[5 + z : 6 + z]
        for m in range(2):
            txp[r, m] = jnp.where(
                tile_row < 5, line[2 * m], pltpu.roll(line[2 * m + 1], 3, axis=0)
            )
        copy(txp.at[r], rxp.at[r], (r, 3), depth_peer(1)).start()

        for z in range(DEPTH - 1, 1, -1):
            which = 0 if z < 4 else 1 if z < 8 else 2
            copy(tx2.at[r, which], rx2.at[r, z], (r, 2), depth_peer(z)).start()

        copy(txp.at[r], rxp.at[r], (r, 3), depth_peer(1)).wait_recv()
        rows = rx2.at[r, pl.ds(2, 14)]
        copy(rows, rows, (r, 2), depth_peer(1)).wait_recv()
        far = []
        for m in range(2):
            both = rxp[r, m]
            far += [both, pltpu.roll(both, 5, axis=0)]
        far_half = [far[0] + far[1], far[2] + far[3]]
        six = tree([rx2[r, z] for z in range(2, 4)])
        seven = tree([rx2[r, z] for z in range(4, 8)])
        eight = tree([rx2[r, z] for z in range(8, 16)])
        products = whole[2:3] + (far_half[0] + far_half[1])[2:3]
        products = products + six + seven + eight
        high = jnp.where(tile_row == 5, six, jnp.where(tile_row == 6, seven, eight))
        for y in range(4):
            base = jnp.where(tile_row == 4, half[1 - y // 2] + far_half[1 - y // 2], high)
            base = jnp.where(tile_row == 3, line[y ^ 1] + far[y ^ 1], base)
            base = jnp.where(tile_row == 2, far[y], base)
            for x in range(4):
                e = 4 * y + x
                tile = jnp.where(tile_row == 1, pair[(e // 2) ^ 1], base)
                tile = jnp.where(tile_row == 0, chip[e ^ 1], tile)
                tile = jnp.where(tile_spare, products, tile)
                tx3[r, e] = tile
                if e == 0:
                    rx3[r, plane] = tile

        for d in range(SLICES - 1, 0, -1):
            copy(tx3.at[r, d >> 1], rx3.at[r, plane], (r, 4), plane_peer(d)).start()

    def local_part(r, vector, parts):
        part = nugget[...] * vector + joined(dot(parts, kernel[...]))
        copy(tx0.at[r], rx0.at[r], (r, 0), plane_peer(1)).wait_recv()
        return part + joined(dot(split(rx0[r]), left_fine[0]))

    def end_round(r, count):
        slots = rx3.at[r, pl.ds(0, 31)]
        copy(slots, slots, (r, 4), plane_peer(1)).wait_recv()
        turned = rx3[r].reshape(256, 128).T
        sibling = jnp.concatenate([turned[:48], turned[48:96]], 1)
        far = joined(dot(split(sibling), order_left[...]))
        spare = turned[96:]
        return far, [
            jnp.concatenate(
                [spare[:, 16 * i : 16 * i + 1], spare[16:, 16 * i + 8 : 16 * i + 9]], 0
            ) * (1.0 / TOTAL)
            for i in range(count)
        ]

    def prepare():
        for i in (0, 1, 2, 3, 5):
            fetches[i].wait()
        order_left[...] = dot(order, levels_above(left_fine, left_coarse)).astype(BF16)
        c8[...] = jnp.zeros_like(c8)
        c8[0:3] = centres[...]

    fetches[7].wait()
    first = right_sides[...]
    parts = start_round(0, first, [total_of(first * first)])

    coords = c8[...]
    c_high = coords.astype(BF16).astype(F32)
    c_mid = (coords - c_high).astype(BF16).astype(F32)
    c_low = coords - c_high - c_mid
    chosen = jnp.where(row == leaf_order[...], 1.0, 0.0).astype(BF16)
    split_coords = jnp.concatenate([c_high, c_mid, c_low, jnp.zeros_like(coords)], 0)
    picked = dot(split_coords.astype(BF16), chosen)
    points = (picked[0:8] + picked[8:16]) + picked[16:24]
    points_t = jnp.concatenate([points, jnp.zeros((120, ROWS), F32)], 0).T
    block = 64
    for start in range(0, ROWS, block):
        distance = jnp.full((block, ROWS), SHAPE_SQUARED, F32)
        for coord in range(3):
            between = points_t[start : start + block, coord : coord + 1] - points[coord : coord + 1]
            distance = distance + between * between
        kernel[start : start + block] = (jnp.sqrt(distance) * (1.0 / ROWS**0.5)).astype(BF16)

    near = local_part(0, first, parts)
    sums_round(0)
    far, (square,) = end_round(0, 1)
    norm = jnp.sqrt(square + EPSILON)
    basis = [first / norm]
    images = [(near + far) / norm]
    gram = [[square / (square + EPSILON)]]
    lanes = lax.broadcasted_iota(jnp.int32, (NRHS, 128), 1)
    table = jnp.zeros((NRHS, 128), F32)

    def orthogonalize(step, dots):
        coeffs, square = dots[:-1], dots[-1]
        count = len(coeffs)
        spread = [sum(gram[i][k] * coeffs[k] for k in range(count)) for i in range(count)]
        for i in range(count):
            square = square - coeffs[i] * (2.0 * coeffs[i] - spread[i])
        square = jnp.maximum(square, 0.0)
        norm = jnp.sqrt(square + EPSILON)
        column = [(coeffs[i] - spread[i]) / norm for i in range(count)]
        for i in range(count):
            gram[i].append(column[i])
        gram.append(column + [square / (square + EPSILON)])
        return coeffs, norm

    def combine(value, coeffs, earlier, norm):
        for coeff, other in zip(coeffs, earlier):
            value = value - coeff * other
        return value / norm

    def record(table, step, coeffs, norm):
        for i, value in enumerate(coeffs + [norm]):
            table = jnp.where(lanes == i * STEPS + step, value, table)
        return table

    for r in range(1, STEPS):
        image = images[-1]
        dots = [total_of(other * image) for other in basis] + [total_of(image * image)]
        parts = start_round(r, image, dots)
        near = local_part(r, image, parts)
        sums_round(r)
        far, dots = end_round(r, len(dots))
        coeffs, norm = orthogonalize(r - 1, dots)
        table = record(table, r - 1, coeffs, norm)
        basis.append(combine(image, coeffs, basis, norm))
        images.append(combine(near + far, coeffs, images, norm))

    image = images[-1]
    dots = [total_of(other * image) for other in basis] + [total_of(image * image)]
    side = jnp.zeros((128, 128), F32)
    lanes_all = lax.broadcasted_iota(jnp.int32, (128, 128), 1)
    zeros = jnp.zeros((32, 1), F32)
    for i in range(3):
        below = dots[2 * i + 1] if i < 2 else jnp.zeros((NRHS, 1), F32)
        side = jnp.where(lanes_all == i, jnp.concatenate([dots[2 * i], below, zeros], 0), side)
    tx4[...] = side.T[:8]

    for d in range(SLICES - 1, 0, -1):
        copy(tx4, rx4.at[d], (STEPS, 0), plane_peer(d)).start()

    slots = rx4.at[pl.ds(1, 31)]
    copy(slots, slots, (STEPS, 0), plane_peer(1)).wait_recv()
    tx5[...] = tree([tx4[...]] + [rx4[d] for d in range(1, SLICES)])

    for z in range(DEPTH - 1, 0, -1):
        copy(tx5, rx5.at[z], (STEPS, 1), depth_peer(z)).start()

    slots = rx5.at[pl.ds(1, 15)]
    copy(slots, slots, (STEPS, 1), depth_peer(1)).wait_recv()
    summed = tree([tx5[...]] + [rx5[z] for z in range(1, DEPTH)]) * (1.0 / TOTAL)
    side = jnp.concatenate([summed, jnp.zeros((120, 128), F32)], 0).T
    dots = [side[48 * (i % 2) : 48 * (i % 2) + 48, i // 2 : i // 2 + 1] for i in range(5)]
    coeffs, norm = orthogonalize(STEPS - 1, dots)
    hess[...] = record(table, STEPS - 1, coeffs, norm)
    out[...] = combine(image, coeffs, basis, norm)

    for r in range(STEPS):
        copy(tx0.at[r], rx0.at[r], (r, 0), plane_peer(1)).wait_send()
        copy(tx1.at[r, pl.ds(1, 31)], rx1.at[r, pl.ds(1, 31)], (r, 1), plane_peer(1)).wait_send()
        rows = rx2.at[r, pl.ds(2, 14)]
        copy(rows, rows, (r, 2), depth_peer(1)).wait_send()
        copy(txp.at[r], rxp.at[r], (r, 3), depth_peer(1)).wait_send()
        slots = rx3.at[r, pl.ds(0, 31)]
        copy(slots, slots, (r, 4), plane_peer(1)).wait_send()
    slots = rx4.at[pl.ds(1, 31)]
    copy(slots, slots, (STEPS, 0), plane_peer(1)).wait_send()
    slots = rx5.at[pl.ds(1, 15)]
    copy(slots, slots, (STEPS, 1), depth_peer(1)).wait_send()


def on_device(
    centres, leaf_order, nugget, left_fine, right_fine, left_coarse, right_coarse, right_sides
):
    vmem = pl.BlockSpec(memory_space=pltpu.VMEM)
    arguments = (
        centres, leaf_order, nugget.reshape(1, ROWS), left_fine, right_fine, left_coarse,
        right_coarse, right_sides,
    )
    basis, table = pl.pallas_call(
        body,
        out_shape=(
            jax.ShapeDtypeStruct((NRHS, ROWS), F32),
            jax.ShapeDtypeStruct((NRHS, 128), F32),
        ),
        in_specs=[pl.BlockSpec(memory_space=pl.ANY)] * 8,
        out_specs=(vmem, vmem),
        scratch_shapes=[pltpu.VMEM(value.shape, value.dtype) for value in arguments] + [
            pltpu.VMEM((8, ROWS), F32),
            pltpu.VMEM((512, ROWS), BF16),
            pltpu.VMEM((512, ROWS), BF16),
            pltpu.VMEM((ROWS, ROWS), BF16),
            pltpu.VMEM((STEPS, NRHS, RANK), F32),
            pltpu.VMEM((STEPS, NRHS, RANK), F32),
            pltpu.VMEM((STEPS, SLICES, 8, 128), F32),
            pltpu.VMEM((STEPS, SLICES, 8, 128), F32),
            pltpu.VMEM((STEPS, 3, 1, 128), F32),
            pltpu.VMEM((STEPS, DEPTH, 1, 128), F32),
            pltpu.VMEM((STEPS, 2, 8, 128), F32),
            pltpu.VMEM((STEPS, 2, 8, 128), F32),
            pltpu.VMEM((STEPS, 16, 8, 128), F32),
            pltpu.VMEM((STEPS, SLICES, 8, 128), F32),
            pltpu.VMEM((8, 128), F32),
            pltpu.VMEM((SLICES, 8, 128), F32),
            pltpu.VMEM((8, 128), F32),
            pltpu.VMEM((DEPTH, 8, 128), F32),
            pltpu.SemaphoreType.DMA((STEPS + 1, 5)),
            pltpu.SemaphoreType.DMA((STEPS + 1, 5)),
            pltpu.SemaphoreType.DMA((8,)),
        ],
        compiler_params=pltpu.CompilerParams(
            collective_id=0, has_side_effects=True, vmem_limit_bytes=60 * 1024 * 1024
        ),
    )(*arguments)
    hessenberg = table[:, : (STEPS + 1) * STEPS].reshape(NRHS, STEPS + 1, STEPS)
    return (basis, hessenberg)


def solution(mesh):
    return jax.shard_map(
        on_device,
        mesh=mesh,
        in_specs=(
            P(None, ("outer", "inner")),
            P(("outer", "inner"), None),
            P(("outer", "inner")),
            P(None, None, ("outer", "inner")),
            P(None, None, ("outer", "inner")),
            P(None, None, ("outer", "inner")),
            P(None, None, ("outer", "inner")),
            P(None, ("outer", "inner")),
        ),
        out_specs=(P(None, ("outer", "inner")), P()),
        check_vma=False,
    )
```

```python
import functools

import jax
import jax.numpy as jnp
from jax import lax
from jax.experimental import pallas as pl
from jax.experimental.pallas import tpu as pltpu
from jax.sharding import PartitionSpec as P

ROWS = 512
RANK = 64
NRHS = 48
STEPS = 4
SLICES = 32
DEPTH = 16
TOTAL = 262144.0
SHAPE_SQUARED = 0.0625
EPSILON = 1e-06
MESH = pl.DeviceIdType.MESH
F32 = jnp.float32
BF16 = jnp.bfloat16


def split(value):
    high = value.astype(BF16)
    low = (value - high.astype(F32)).astype(BF16)
    return jnp.concatenate([high, low], 0)


def joined(value):
    return value[:NRHS] + value[NRHS:]


def dot(left, right):
    return jnp.dot(left, right, preferred_element_type=F32)


def dot_t(left, right):
    return lax.dot_general(left, right, (((1,), (1,)), ((), ())), preferred_element_type=F32)


def total_of(value):
    return jnp.sum(value, axis=1, keepdims=True)


def tree(values):
    values = list(values)
    while len(values) > 1:
        values = [values[i] + values[i + 1] for i in range(0, len(values), 2)]
    return values[0]


def body(*refs):
    sources, refs = refs[:8], refs[8:]
    both = refs[0]
    held, refs = refs[1:9], refs[9:]
    centres, leaf_order, nugget, left_fine, right_fine, left_coarse, right_coarse, right_sides = held
    (
        c8, order_right, order_left, kernel, tx0, rx0, tx1, rx1, tx2, rx2, txp, rxp, tx3, rx3,
        tx4, rx4, tx5, rx5, send, recv, fetched,
    ) = refs
    fetches = [
        pltpu.make_async_copy(sources[i], held[i], fetched.at[i]) for i in range(8)
    ]
    for i in (4, 6, 7, 3, 5, 1, 0, 2):
        fetches[i].start()
    inner, outer = lax.axis_index("inner"), lax.axis_index("outer")
    plane = (outer % 4) * 8 + inner % 8

    def plane_peer(d):
        return {"inner": inner ^ (d & 7), "outer": outer ^ (d >> 3)}

    def depth_peer(z):
        return {"inner": inner ^ ((z & 1) << 3), "outer": outer ^ ((z >> 1) << 2)}

    def copy(src, dst, sems, peer):
        return pltpu.make_async_remote_copy(
            src_ref=src, dst_ref=dst, send_sem=send.at[sems], recv_sem=recv.at[sems],
            device_id=peer, device_id_type=MESH,
        )

    barrier = pltpu.get_barrier_semaphore()

    for z in range(1, DEPTH):
        pl.semaphore_signal(barrier, inc=1, device_id=depth_peer(z), device_id_type=MESH)
    for d in range(SLICES - 1, 0, -1):
        pl.semaphore_signal(barrier, inc=1, device_id=plane_peer(d), device_id_type=MESH)

    row = lax.broadcasted_iota(jnp.int32, (512, 512), 0)
    col = lax.broadcasted_iota(jnp.int32, (512, 512), 1)
    wanted = (row & 7) * RANK + ((row & 255) >> 3) * 2 + (row >> 8)
    order = jnp.where(wanted == col, 1.0, 0.0).astype(BF16)

    def levels_above(fine, coarse):
        return jnp.concatenate(
            [fine[1:].reshape(3 * RANK, ROWS), coarse[...].reshape(5 * RANK, ROWS)], 0
        )

    fetches[4].wait()
    fetches[6].wait()
    order_right[...] = dot(order, levels_above(right_fine, right_coarse)).T.astype(BF16)

    lane = lax.broadcasted_iota(jnp.int32, (32, 256), 1)
    spare_dot, spare_odd = (lane >> 4) & 7, ((lane >> 3) & 1) == 1
    tile_row = lax.broadcasted_iota(jnp.int32, (8, 128), 0)
    tile_spare = lax.broadcasted_iota(jnp.int32, (8, 128), 1) >= 96

    def start_round(r, vector, dots):
        parts = split(vector)
        terms = joined(dot(parts, order_right[...]))
        spare = jnp.zeros((32, 256), F32)
        for i, value in enumerate(dots):
            spare = jnp.where(
                spare_dot == i, jnp.where(spare_odd, value[16:48], value[0:32]), spare
            )
        tiles = jnp.concatenate([terms[:, :256], terms[:, 256:], spare], 0).T
        tx1[r] = tiles.reshape(SLICES, 8, 128)
        if r == 0:
            prepare()
            pl.semaphore_wait(barrier, SLICES + DEPTH - 2)
        for d in range(SLICES - 1, 0, -1):
            copy(tx1.at[r, plane ^ d], rx1.at[r, d], (r, 1), plane_peer(d)).start()

        tx0[r] = joined(dot_t(parts, right_fine[0]))
        copy(tx0.at[r], rx0.at[r], (r, 0), plane_peer(1)).start()
        return parts

    def sums_round(r):
        copy(tx1.at[r, pl.ds(1, 31)], rx1.at[r, pl.ds(1, 31)], (r, 1), plane_peer(1)).wait_recv()
        own = tx1[r, plane]
        chip = [own + rx1[r, 1]] + [rx1[r, 2 * e] + rx1[r, 2 * e + 1] for e in range(1, 16)]
        pair = [chip[2 * h] + chip[2 * h + 1] for h in range(8)]
        line = [pair[2 * y] + pair[2 * y + 1] for y in range(4)]
        half = [line[0] + line[1], line[2] + line[3]]
        whole = half[0] + half[1]
        for z in range(3):
            tx2[r, z] = whole[5 + z : 6 + z]
        for y in range(4):
            txp[r, y] = line[y][2:3]
            txp[r, 4 + y] = line[y][3:4]
        for m in range(2):
            txp[r, 8 + m] = half[m][4:5]
        copy(txp.at[r], rxp.at[r], (r, 3), depth_peer(1)).start()

        for z in range(DEPTH - 1, 1, -1):
            which = 0 if z < 4 else 1 if z < 8 else 2
            copy(tx2.at[r, which], rx2.at[r, z], (r, 2), depth_peer(z)).start()

        copy(txp.at[r], rxp.at[r], (r, 3), depth_peer(1)).wait_recv()
        rows = rx2.at[r, pl.ds(2, 14)]
        copy(rows, rows, (r, 2), depth_peer(1)).wait_recv()
        six = tree([rx2[r, z] for z in range(2, 4)])
        seven = tree([rx2[r, z] for z in range(4, 8)])
        eight = tree([rx2[r, z] for z in range(8, 16)])
        products = whole[2:3] + tree([rxp[r, y] for y in range(4)])
        products = products + six + seven + eight
        high = jnp.where(tile_row == 5, six, jnp.where(tile_row == 6, seven, eight))
        for y in range(4):
            base = jnp.where(tile_row == 4, half[1 - y // 2] + rxp[r, 9 - y // 2], high)
            base = jnp.where(tile_row == 3, line[y ^ 1] + rxp[r, 4 + (y ^ 1)], base)
            base = jnp.where(tile_row == 2, rxp[r, y], base)
            for x in range(4):
                e = 4 * y + x
                tile = jnp.where(tile_row == 1, pair[(e // 2) ^ 1], base)
                tile = jnp.where(tile_row == 0, chip[e ^ 1], tile)
                tile = jnp.where(tile_spare, products, tile)
                tx3[r, e] = tile
                if e == 0:
                    rx3[r, plane] = tile

        for d in range(SLICES - 1, 0, -1):
            copy(tx3.at[r, d >> 1], rx3.at[r, plane], (r, 4), plane_peer(d)).start()

    def local_part(r, vector, parts):
        part = nugget[...] * vector + joined(dot(parts, kernel[...]))
        copy(tx0.at[r], rx0.at[r], (r, 0), plane_peer(1)).wait_recv()
        return part + joined(dot(split(rx0[r]), left_fine[0]))

    def end_round(r, count):
        slots = rx3.at[r, pl.ds(0, 31)]
        copy(slots, slots, (r, 4), plane_peer(1)).wait_recv()
        turned = rx3[r].reshape(256, 128).T
        sibling = jnp.concatenate([turned[:48], turned[48:96]], 1)
        far = joined(dot(split(sibling), order_left[...]))
        spare = turned[96:]
        return far, [
            jnp.concatenate(
                [spare[:, 16 * i : 16 * i + 1], spare[16:, 16 * i + 8 : 16 * i + 9]], 0
            ) * (1.0 / TOTAL)
            for i in range(count)
        ]

    def prepare():
        for i in (0, 1, 2, 3, 5):
            fetches[i].wait()
        order_left[...] = dot(order, levels_above(left_fine, left_coarse)).astype(BF16)
        c8[...] = jnp.zeros_like(c8)
        c8[0:3] = centres[...]

    fetches[7].wait()
    first = right_sides[...]
    parts = start_round(0, first, [total_of(first * first)])

    coords = c8[...]
    c_high = coords.astype(BF16).astype(F32)
    c_mid = (coords - c_high).astype(BF16).astype(F32)
    c_low = coords - c_high - c_mid
    chosen = jnp.where(row == leaf_order[...], 1.0, 0.0).astype(BF16)
    split_coords = jnp.concatenate([c_high, c_mid, c_low, jnp.zeros_like(coords)], 0)
    picked = dot(split_coords.astype(BF16), chosen)
    points = (picked[0:8] + picked[8:16]) + picked[16:24]
    points_t = jnp.concatenate([points, jnp.zeros((120, ROWS), F32)], 0).T
    block = 64
    for start in range(0, ROWS, block):
        distance = jnp.full((block, ROWS), SHAPE_SQUARED, F32)
        for coord in range(3):
            between = points_t[start : start + block, coord : coord + 1] - points[coord : coord + 1]
            distance = distance + between * between
        kernel[start : start + block] = (jnp.sqrt(distance) * (1.0 / ROWS**0.5)).astype(BF16)

    near = local_part(0, first, parts)
    sums_round(0)
    far, (square,) = end_round(0, 1)
    scale = 1.0 / jnp.sqrt(square + EPSILON)
    basis = [first * scale]
    images = [(near + far) * scale]
    gram = [[square / (square + EPSILON)]]
    lanes = lax.broadcasted_iota(jnp.int32, (NRHS, 128), 1)
    table = jnp.zeros((NRHS, 128), F32)

    def orthogonalize(step, dots):
        coeffs, square = dots[:-1], dots[-1]
        count = len(coeffs)
        spread = [sum(gram[i][k] * coeffs[k] for k in range(count)) for i in range(count)]
        for i in range(count):
            square = square - coeffs[i] * (2.0 * coeffs[i] - spread[i])
        square = jnp.maximum(square, 0.0)
        norm = jnp.sqrt(square + EPSILON)
        scale = 1.0 / norm
        column = [(coeffs[i] - spread[i]) * scale for i in range(count)]
        for i in range(count):
            gram[i].append(column[i])
        gram.append(column + [square / (square + EPSILON)])
        return coeffs, norm, scale

    def combine(value, coeffs, earlier, scale):
        for coeff, other in zip(coeffs, earlier):
            value = value - coeff * other
        return value * scale

    def record(table, step, coeffs, norm):
        for i, value in enumerate(coeffs + [norm]):
            table = jnp.where(lanes == i * STEPS + step, value, table)
        return table

    for r in range(1, STEPS):
        image = images[-1]
        dots = [total_of(other * image) for other in basis] + [total_of(image * image)]
        parts = start_round(r, image, dots)
        near = local_part(r, image, parts)
        sums_round(r)
        far, dots = end_round(r, len(dots))
        coeffs, norm, scale = orthogonalize(r - 1, dots)
        table = record(table, r - 1, coeffs, norm)
        basis.append(combine(image, coeffs, basis, scale))
        images.append(combine(near + far, coeffs, images, scale))

    image = images[-1]
    dots = [total_of(other * image) for other in basis] + [total_of(image * image)]
    side = jnp.zeros((128, 128), F32)
    lanes_all = lax.broadcasted_iota(jnp.int32, (128, 128), 1)
    zeros = jnp.zeros((32, 1), F32)
    for i in range(3):
        below = dots[2 * i + 1] if i < 2 else jnp.zeros((NRHS, 1), F32)
        side = jnp.where(lanes_all == i, jnp.concatenate([dots[2 * i], below, zeros], 0), side)
    tx4[...] = side.T[:4]

    for d in range(SLICES - 1, 0, -1):
        copy(tx4, rx4.at[d], (STEPS, 0), plane_peer(d)).start()

    slots = rx4.at[pl.ds(1, 31)]
    copy(slots, slots, (STEPS, 0), plane_peer(1)).wait_recv()
    tx5[...] = tree([tx4[...]] + [rx4[d] for d in range(1, SLICES)])

    for z in range(DEPTH - 1, 0, -1):
        copy(tx5, rx5.at[z], (STEPS, 1), depth_peer(z)).start()

    slots = rx5.at[pl.ds(1, 15)]
    copy(slots, slots, (STEPS, 1), depth_peer(1)).wait_recv()
    summed = tree([tx5[...]] + [rx5[z] for z in range(1, DEPTH)]) * (1.0 / TOTAL)
    side = jnp.concatenate([summed, jnp.zeros((124, 128), F32)], 0).T
    dots = [side[48 * (i % 2) : 48 * (i % 2) + 48, i // 2 : i // 2 + 1] for i in range(5)]
    coeffs, norm, scale = orthogonalize(STEPS - 1, dots)
    both[:, ROWS:] = record(table, STEPS - 1, coeffs, norm)
    both[:, :ROWS] = combine(image, coeffs, basis, scale)

    for r in range(STEPS):
        copy(tx0.at[r], rx0.at[r], (r, 0), plane_peer(1)).wait_send()
        copy(tx1.at[r, pl.ds(1, 31)], rx1.at[r, pl.ds(1, 31)], (r, 1), plane_peer(1)).wait_send()
        rows = rx2.at[r, pl.ds(2, 14)]
        copy(rows, rows, (r, 2), depth_peer(1)).wait_send()
        copy(txp.at[r], rxp.at[r], (r, 3), depth_peer(1)).wait_send()
        slots = rx3.at[r, pl.ds(0, 31)]
        copy(slots, slots, (r, 4), plane_peer(1)).wait_send()
    slots = rx4.at[pl.ds(1, 31)]
    copy(slots, slots, (STEPS, 0), plane_peer(1)).wait_send()
    slots = rx5.at[pl.ds(1, 15)]
    copy(slots, slots, (STEPS, 1), depth_peer(1)).wait_send()


def on_device(
    centres, leaf_order, nugget, left_fine, right_fine, left_coarse, right_coarse, right_sides
):
    vmem = pl.BlockSpec(memory_space=pltpu.VMEM)
    arguments = (
        centres, leaf_order, nugget.reshape(1, ROWS), left_fine, right_fine, left_coarse,
        right_coarse, right_sides,
    )
    both = pl.pallas_call(
        body,
        out_shape=jax.ShapeDtypeStruct((NRHS, ROWS + 128), F32),
        in_specs=[pl.BlockSpec(memory_space=pl.ANY)] * 8,
        out_specs=vmem,
        scratch_shapes=[pltpu.VMEM(value.shape, value.dtype) for value in arguments] + [
            pltpu.VMEM((8, ROWS), F32),
            pltpu.VMEM((512, ROWS), BF16),
            pltpu.VMEM((512, ROWS), BF16),
            pltpu.VMEM((ROWS, ROWS), BF16),
            pltpu.VMEM((STEPS, NRHS, RANK), F32),
            pltpu.VMEM((STEPS, NRHS, RANK), F32),
            pltpu.VMEM((STEPS, SLICES, 8, 128), F32),
            pltpu.VMEM((STEPS, SLICES, 8, 128), F32),
            pltpu.VMEM((STEPS, 3, 1, 128), F32),
            pltpu.VMEM((STEPS, DEPTH, 1, 128), F32),
            pltpu.VMEM((STEPS, 10, 1, 128), F32),
            pltpu.VMEM((STEPS, 10, 1, 128), F32),
            pltpu.VMEM((STEPS, 16, 8, 128), F32),
            pltpu.VMEM((STEPS, SLICES, 8, 128), F32),
            pltpu.VMEM((4, 128), F32),
            pltpu.VMEM((SLICES, 4, 128), F32),
            pltpu.VMEM((4, 128), F32),
            pltpu.VMEM((DEPTH, 4, 128), F32),
            pltpu.SemaphoreType.DMA((STEPS + 1, 5)),
            pltpu.SemaphoreType.DMA((STEPS + 1, 5)),
            pltpu.SemaphoreType.DMA((8,)),
        ],
        compiler_params=pltpu.CompilerParams(
            collective_id=0, has_side_effects=True, vmem_limit_bytes=60 * 1024 * 1024
        ),
    )(*arguments)
    table = both[:, ROWS : ROWS + (STEPS + 1) * STEPS]
    return (both[:, :ROWS], table.reshape(NRHS, STEPS + 1, STEPS))


def solution(mesh):
    return jax.shard_map(
        on_device,
        mesh=mesh,
        in_specs=(
            P(None, ("outer", "inner")),
            P(("outer", "inner"), None),
            P(("outer", "inner")),
            P(None, None, ("outer", "inner")),
            P(None, None, ("outer", "inner")),
            P(None, None, ("outer", "inner")),
            P(None, None, ("outer", "inner")),
            P(None, ("outer", "inner")),
        ),
        out_specs=(P(None, ("outer", "inner")), P()),
        check_vma=False,
    )
```

```python
import functools

import jax
import jax.numpy as jnp
from jax import lax
from jax.experimental import pallas as pl
from jax.experimental.pallas import tpu as pltpu
from jax.sharding import PartitionSpec as P

ROWS = 512
RANK = 64
NRHS = 48
STEPS = 4
SLICES = 32
DEPTH = 16
TOTAL = 262144.0
SHAPE_SQUARED = 0.0625
EPSILON = 1e-06
MESH = pl.DeviceIdType.MESH
F32 = jnp.float32
BF16 = jnp.bfloat16


def split(value):
    high = value.astype(BF16)
    low = (value - high.astype(F32)).astype(BF16)
    return jnp.concatenate([high, low], 0)


def joined(value):
    return value[:NRHS] + value[NRHS:]


def dot(left, right):
    return jnp.dot(left, right, preferred_element_type=F32)


def dot_t(left, right):
    return lax.dot_general(left, right, (((1,), (1,)), ((), ())), preferred_element_type=F32)


def total_of(value):
    return jnp.sum(value, axis=1, keepdims=True)


def tree(values):
    values = list(values)
    while len(values) > 1:
        values = [values[i] + values[i + 1] for i in range(0, len(values), 2)]
    return values[0]


def body(*refs):
    sources, refs = refs[:8], refs[8:]
    both = refs[0]
    held, refs = refs[1:9], refs[9:]
    centres, leaf_order, nugget, left_fine, right_fine, left_coarse, right_coarse, right_sides = held
    (
        c8, order_right, order_left, kernel, tx0, rx0, tx1, rx1, tx2, rx2, txp, rxp, tx3, rx3,
        tx4, rx4, tx5, rx5, send, recv, fetched,
    ) = refs
    fetches = [
        pltpu.make_async_copy(sources[i], held[i], fetched.at[i]) for i in range(8)
    ]
    for i in (4, 6, 7, 3, 5, 1, 0, 2):
        fetches[i].start()
    inner, outer = lax.axis_index("inner"), lax.axis_index("outer")
    plane = (outer % 4) * 8 + inner % 8

    def plane_peer(d):
        return {"inner": inner ^ (d & 7), "outer": outer ^ (d >> 3)}

    def depth_peer(z):
        return {"inner": inner ^ ((z & 1) << 3), "outer": outer ^ ((z >> 1) << 2)}

    def copy(src, dst, sems, peer):
        return pltpu.make_async_remote_copy(
            src_ref=src, dst_ref=dst, send_sem=send.at[sems], recv_sem=recv.at[sems],
            device_id=peer, device_id_type=MESH,
        )

    barrier = pltpu.get_barrier_semaphore()

    for z in range(1, DEPTH):
        pl.semaphore_signal(barrier, inc=1, device_id=depth_peer(z), device_id_type=MESH)
    for d in range(SLICES - 1, 0, -1):
        pl.semaphore_signal(barrier, inc=1, device_id=plane_peer(d), device_id_type=MESH)

    row = lax.broadcasted_iota(jnp.int32, (512, 512), 0)
    col = lax.broadcasted_iota(jnp.int32, (512, 512), 1)
    wanted = (row & 7) * RANK + ((row & 255) >> 3) * 2 + (row >> 8)
    order = jnp.where(wanted == col, 1.0, 0.0).astype(BF16)

    def levels_above(fine, coarse):
        return jnp.concatenate(
            [fine[1:].reshape(3 * RANK, ROWS), coarse[...].reshape(5 * RANK, ROWS)], 0
        )

    fetches[4].wait()
    fetches[6].wait()
    order_right[...] = dot(order, levels_above(right_fine, right_coarse)).T.astype(BF16)

    lane = lax.broadcasted_iota(jnp.int32, (32, 256), 1)
    spare_dot, spare_odd = (lane >> 4) & 7, ((lane >> 3) & 1) == 1
    tile_row = lax.broadcasted_iota(jnp.int32, (8, 128), 0)
    tile_spare = lax.broadcasted_iota(jnp.int32, (8, 128), 1) >= 96

    def start_round(r, vector, dots):
        parts = split(vector)
        terms = joined(dot(parts, order_right[...]))
        spare = jnp.zeros((32, 256), F32)
        for i, value in enumerate(dots):
            spare = jnp.where(
                spare_dot == i, jnp.where(spare_odd, value[16:48], value[0:32]), spare
            )
        tiles = jnp.concatenate([terms[:, :256], terms[:, 256:], spare], 0).T
        tx1[r] = tiles.reshape(SLICES, 8, 128)
        if r == 0:
            prepare()
            pl.semaphore_wait(barrier, SLICES + DEPTH - 2)
        for d in range(SLICES - 1, 0, -1):
            copy(tx1.at[r, plane ^ d], rx1.at[r, d], (r, 1), plane_peer(d)).start()

        tx0[r] = joined(dot_t(parts, right_fine[0]))
        copy(tx0.at[r], rx0.at[r], (r, 0), plane_peer(1)).start()
        return parts

    def sums_round(r):
        copy(tx1.at[r, pl.ds(1, 31)], rx1.at[r, pl.ds(1, 31)], (r, 1), plane_peer(1)).wait_recv()
        own = tx1[r, plane]
        chip = [own + rx1[r, 1]] + [rx1[r, 2 * e] + rx1[r, 2 * e + 1] for e in range(1, 16)]
        pair = [chip[2 * h] + chip[2 * h + 1] for h in range(8)]
        line = [pair[2 * y] + pair[2 * y + 1] for y in range(4)]
        half = [line[0] + line[1], line[2] + line[3]]
        for y in range(4):
            txp[r, y] = line[y][2:3]
            txp[r, 4 + y] = line[y][3:4]
        for m in range(2):
            txp[r, 8 + m] = half[m][4:5]
        copy(txp.at[r], rxp.at[r], (r, 3), depth_peer(1)).start()
        whole = half[0] + half[1]
        for z in range(3):
            tx2[r, z] = whole[5 + z : 6 + z]
        for z in range(DEPTH - 1, 1, -1):
            which = 0 if z < 4 else 1 if z < 8 else 2
            copy(tx2.at[r, which], rx2.at[r, z], (r, 2), depth_peer(z)).start()

        lows = [jnp.where(tile_row == 0, chip[e ^ 1], pair[(e // 2) ^ 1]) for e in range(16)]
        low = (tile_row < 2) & ~tile_spare
        copy(txp.at[r], rxp.at[r], (r, 3), depth_peer(1)).wait_recv()
        rows = rx2.at[r, pl.ds(2, 14)]
        copy(rows, rows, (r, 2), depth_peer(1)).wait_recv()
        six = tree([rx2[r, z] for z in range(2, 4)])
        seven = tree([rx2[r, z] for z in range(4, 8)])
        eight = tree([rx2[r, z] for z in range(8, 16)])
        products = whole[2:3] + tree([rxp[r, y] for y in range(4)])
        products = products + six + seven + eight
        high = jnp.where(tile_row == 5, six, jnp.where(tile_row == 6, seven, eight))
        for y in range(3, -1, -1):
            base = jnp.where(tile_row == 4, half[1 - y // 2] + rxp[r, 9 - y // 2], high)
            base = jnp.where(tile_row == 3, line[y ^ 1] + rxp[r, 4 + (y ^ 1)], base)
            base = jnp.where(tile_row == 2, rxp[r, y], base)
            base = jnp.where(tile_spare, products, base)
            for x in range(3, -1, -1):
                e = 4 * y + x
                tile = jnp.where(low, lows[e], base)
                tx3[r, e] = tile
                if e == 0:
                    rx3[r, plane] = tile
                for d in (2 * e + 1, 2 * e)[: 2 if e else 1]:
                    copy(tx3.at[r, e], rx3.at[r, plane], (r, 4), plane_peer(d)).start()

    def local_part(r, vector, parts):
        part = nugget[...] * vector + joined(dot(parts, kernel[...]))
        copy(tx0.at[r], rx0.at[r], (r, 0), plane_peer(1)).wait_recv()
        return part + joined(dot(split(rx0[r]), left_fine[0]))

    def end_round(r, count):
        slots = rx3.at[r, pl.ds(0, 31)]
        copy(slots, slots, (r, 4), plane_peer(1)).wait_recv()
        turned = rx3[r].reshape(256, 128).T
        sibling = jnp.concatenate([turned[:48], turned[48:96]], 1)
        far = joined(dot(split(sibling), order_left[...]))
        spare = turned[96:]
        return far, [
            jnp.concatenate(
                [spare[:, 16 * i : 16 * i + 1], spare[16:, 16 * i + 8 : 16 * i + 9]], 0
            ) * (1.0 / TOTAL)
            for i in range(count)
        ]

    def prepare():
        for i in (0, 1, 2, 3, 5):
            fetches[i].wait()
        order_left[...] = dot(order, levels_above(left_fine, left_coarse)).astype(BF16)
        c8[...] = jnp.zeros_like(c8)
        c8[0:3] = centres[...]

    fetches[7].wait()
    first = right_sides[...]
    parts = start_round(0, first, [total_of(first * first)])

    coords = c8[...]
    c_high = coords.astype(BF16).astype(F32)
    c_mid = (coords - c_high).astype(BF16).astype(F32)
    c_low = coords - c_high - c_mid
    chosen = jnp.where(row == leaf_order[...], 1.0, 0.0).astype(BF16)
    split_coords = jnp.concatenate([c_high, c_mid, c_low, jnp.zeros_like(coords)], 0)
    picked = dot(split_coords.astype(BF16), chosen)
    points = (picked[0:8] + picked[8:16]) + picked[16:24]
    points_t = jnp.concatenate([points, jnp.zeros((120, ROWS), F32)], 0).T
    block = 64
    for start in range(0, ROWS, block):
        distance = jnp.full((block, ROWS), SHAPE_SQUARED, F32)
        for coord in range(3):
            between = points_t[start : start + block, coord : coord + 1] - points[coord : coord + 1]
            distance = distance + between * between
        kernel[start : start + block] = (jnp.sqrt(distance) * (1.0 / ROWS**0.5)).astype(BF16)

    near = local_part(0, first, parts)
    sums_round(0)
    far, (square,) = end_round(0, 1)
    scale = 1.0 / jnp.sqrt(square + EPSILON)
    basis = [first * scale]
    images = [(near + far) * scale]
    gram = [[square / (square + EPSILON)]]
    lanes = lax.broadcasted_iota(jnp.int32, (NRHS, 128), 1)
    table = jnp.zeros((NRHS, 128), F32)

    def orthogonalize(step, dots):
        coeffs, square = dots[:-1], dots[-1]
        count = len(coeffs)
        spread = [sum(gram[i][k] * coeffs[k] for k in range(count)) for i in range(count)]
        for i in range(count):
            square = square - coeffs[i] * (2.0 * coeffs[i] - spread[i])
        square = jnp.maximum(square, 0.0)
        norm = jnp.sqrt(square + EPSILON)
        scale = 1.0 / norm
        column = [(coeffs[i] - spread[i]) * scale for i in range(count)]
        for i in range(count):
            gram[i].append(column[i])
        gram.append(column + [square / (square + EPSILON)])
        return coeffs, norm, scale

    def combine(value, coeffs, earlier, scale):
        for coeff, other in zip(coeffs, earlier):
            value = value - coeff * other
        return value * scale

    def record(table, step, coeffs, norm):
        for i, value in enumerate(coeffs + [norm]):
            table = jnp.where(lanes == i * STEPS + step, value, table)
        return table

    for r in range(1, STEPS):
        image = images[-1]
        dots = [total_of(other * image) for other in basis] + [total_of(image * image)]
        parts = start_round(r, image, dots)
        near = local_part(r, image, parts)
        sums_round(r)
        far, dots = end_round(r, len(dots))
        coeffs, norm, scale = orthogonalize(r - 1, dots)
        table = record(table, r - 1, coeffs, norm)
        basis.append(combine(image, coeffs, basis, scale))
        images.append(combine(near + far, coeffs, images, scale))

    image = images[-1]
    dots = [total_of(other * image) for other in basis] + [total_of(image * image)]
    side = jnp.zeros((128, 128), F32)
    lanes_all = lax.broadcasted_iota(jnp.int32, (128, 128), 1)
    zeros = jnp.zeros((32, 1), F32)
    for i in range(3):
        below = dots[2 * i + 1] if i < 2 else jnp.zeros((NRHS, 1), F32)
        side = jnp.where(lanes_all == i, jnp.concatenate([dots[2 * i], below, zeros], 0), side)
    tx4[...] = side.T[:4]

    for d in range(SLICES - 1, 0, -1):
        copy(tx4, rx4.at[d], (STEPS, 0), plane_peer(d)).start()

    slots = rx4.at[pl.ds(1, 31)]
    copy(slots, slots, (STEPS, 0), plane_peer(1)).wait_recv()
    tx5[...] = tree([tx4[...]] + [rx4[d] for d in range(1, SLICES)])

    for z in range(DEPTH - 1, 0, -1):
        copy(tx5, rx5.at[z], (STEPS, 1), depth_peer(z)).start()

    slots = rx5.at[pl.ds(1, 15)]
    copy(slots, slots, (STEPS, 1), depth_peer(1)).wait_recv()
    summed = tree([tx5[...]] + [rx5[z] for z in range(1, DEPTH)]) * (1.0 / TOTAL)
    side = jnp.concatenate([summed, jnp.zeros((124, 128), F32)], 0).T
    dots = [side[48 * (i % 2) : 48 * (i % 2) + 48, i // 2 : i // 2 + 1] for i in range(5)]
    coeffs, norm, scale = orthogonalize(STEPS - 1, dots)
    both[:, ROWS:] = record(table, STEPS - 1, coeffs, norm)
    both[:, :ROWS] = combine(image, coeffs, basis, scale)

    for r in range(STEPS):
        copy(tx0.at[r], rx0.at[r], (r, 0), plane_peer(1)).wait_send()
        copy(tx1.at[r, pl.ds(1, 31)], rx1.at[r, pl.ds(1, 31)], (r, 1), plane_peer(1)).wait_send()
        rows = rx2.at[r, pl.ds(2, 14)]
        copy(rows, rows, (r, 2), depth_peer(1)).wait_send()
        copy(txp.at[r], rxp.at[r], (r, 3), depth_peer(1)).wait_send()
        slots = rx3.at[r, pl.ds(0, 31)]
        copy(slots, slots, (r, 4), plane_peer(1)).wait_send()
    slots = rx4.at[pl.ds(1, 31)]
    copy(slots, slots, (STEPS, 0), plane_peer(1)).wait_send()
    slots = rx5.at[pl.ds(1, 15)]
    copy(slots, slots, (STEPS, 1), depth_peer(1)).wait_send()


def on_device(
    centres, leaf_order, nugget, left_fine, right_fine, left_coarse, right_coarse, right_sides
):
    vmem = pl.BlockSpec(memory_space=pltpu.VMEM)
    arguments = (
        centres, leaf_order, nugget.reshape(1, ROWS), left_fine, right_fine, left_coarse,
        right_coarse, right_sides,
    )
    both = pl.pallas_call(
        body,
        out_shape=jax.ShapeDtypeStruct((NRHS, ROWS + 128), F32),
        in_specs=[pl.BlockSpec(memory_space=pl.ANY)] * 8,
        out_specs=vmem,
        scratch_shapes=[pltpu.VMEM(value.shape, value.dtype) for value in arguments] + [
            pltpu.VMEM((8, ROWS), F32),
            pltpu.VMEM((512, ROWS), BF16),
            pltpu.VMEM((512, ROWS), BF16),
            pltpu.VMEM((ROWS, ROWS), BF16),
            pltpu.VMEM((STEPS, NRHS, RANK), F32),
            pltpu.VMEM((STEPS, NRHS, RANK), F32),
            pltpu.VMEM((STEPS, SLICES, 8, 128), F32),
            pltpu.VMEM((STEPS, SLICES, 8, 128), F32),
            pltpu.VMEM((STEPS, 3, 1, 128), F32),
            pltpu.VMEM((STEPS, DEPTH, 1, 128), F32),
            pltpu.VMEM((STEPS, 10, 1, 128), F32),
            pltpu.VMEM((STEPS, 10, 1, 128), F32),
            pltpu.VMEM((STEPS, 16, 8, 128), F32),
            pltpu.VMEM((STEPS, SLICES, 8, 128), F32),
            pltpu.VMEM((4, 128), F32),
            pltpu.VMEM((SLICES, 4, 128), F32),
            pltpu.VMEM((4, 128), F32),
            pltpu.VMEM((DEPTH, 4, 128), F32),
            pltpu.SemaphoreType.DMA((STEPS + 1, 5)),
            pltpu.SemaphoreType.DMA((STEPS + 1, 5)),
            pltpu.SemaphoreType.DMA((8,)),
        ],
        compiler_params=pltpu.CompilerParams(
            collective_id=0, has_side_effects=True, vmem_limit_bytes=60 * 1024 * 1024
        ),
    )(*arguments)
    table = both[:, ROWS : ROWS + (STEPS + 1) * STEPS]
    return (both[:, :ROWS], table.reshape(NRHS, STEPS + 1, STEPS))


def solution(mesh):
    return jax.shard_map(
        on_device,
        mesh=mesh,
        in_specs=(
            P(None, ("outer", "inner")),
            P(("outer", "inner"), None),
            P(("outer", "inner")),
            P(None, None, ("outer", "inner")),
            P(None, None, ("outer", "inner")),
            P(None, None, ("outer", "inner")),
            P(None, None, ("outer", "inner")),
            P(None, ("outer", "inner")),
        ),
        out_specs=(P(None, ("outer", "inner")), P()),
        check_vma=False,
    )
```
